32 devices in a mesh: dp: 4 (over y, x), fsdp: 8 (over z, core).
Axes of the slice: x: 2, y: 2, z: 4, core: 2. Of those that a mesh axis runs over, the one named last changes fastest.
Arguments:
- tokens: bfloat16 [8192, 768], P(('dp', 'fsdp')), may hold values from -6 to 6
- keep_pos: int32 [32, 256], P(('dp', 'fsdp')), may hold values from 0 to 1024, as said below
- bucket: int32 [32], P(('dp', 'fsdp')), may hold values from 0 to 1, as said below
- cotangent: bfloat16 [32768, 512], P(('dp', 'fsdp')), may hold values from -6 to 6
- enc_gain1: bfloat16 [768], P(('dp', 'fsdp')), may hold values from 0.5 to 1.5
- enc_shift1: bfloat16 [768], P(('dp', 'fsdp')), may hold values from -2 to 2
- enc_qkv: bfloat16 [768, 2304], P(('dp', 'fsdp')), may hold values from -0.3125 to 0.3125
- enc_proj: bfloat16 [768, 768], P(('dp', 'fsdp')), may hold values from -0.625 to 0.625
- enc_gain2: bfloat16 [768], P(('dp', 'fsdp')), may hold values from 0.5 to 1.5
- enc_shift2: bfloat16 [768], P(('dp', 'fsdp')), may hold values from -2 to 2
- enc_up: bfloat16 [768, 3072], P(('dp', 'fsdp')), may hold values from -0.21875 to 0.21875
- enc_down: bfloat16 [3072, 768], P(('dp', 'fsdp')), may hold values from -0.15625 to 0.15625
- embedding: bfloat16 [768, 512], P(('dp', 'fsdp')), may hold values from -0.21875 to 0.21875
- mask_token: bfloat16 [512], P(('dp', 'fsdp')), may hold values from -4 to 4
- dec_gain1: bfloat16 [512], P(('dp', 'fsdp')), may hold values from 0.5 to 1.5
- dec_shift1: bfloat16 [512], P(('dp', 'fsdp')), may hold values from -2 to 2
- dec_qkv: bfloat16 [512, 1536], P(('dp', 'fsdp')), may hold values from -0.375 to 0.375
- dec_proj: bfloat16 [512, 512], P(('dp', 'fsdp')), may hold values from -0.75 to 0.75
- dec_gain2: bfloat16 [512], P(('dp', 'fsdp')), may hold values from 0.5 to 1.5
- dec_shift2: bfloat16 [512], P(('dp', 'fsdp')), may hold values from -2 to 2
- dec_up: bfloat16 [512, 2048], P(('dp', 'fsdp')), may hold values from -0.25 to 0.25
- dec_down: bfloat16 [2048, 512], P(('dp', 'fsdp')), may hold values from -0.1875 to 0.1875
Outputs:
- output: bfloat16 [32768, 512], P(('dp', 'fsdp'))
- grad_tokens: float32 [8192, 768], P(('dp', 'fsdp'))
- grad_enc_gain1: float32 [768], P(('dp', 'fsdp'))
- grad_enc_shift1: float32 [768], P(('dp', 'fsdp'))
- grad_enc_qkv: float32 [768, 2304], P(('dp', 'fsdp'))
- grad_enc_proj: float32 [768, 768], P(('dp', 'fsdp'))
- grad_enc_gain2: float32 [768], P(('dp', 'fsdp'))
- grad_enc_shift2: float32 [768], P(('dp', 'fsdp'))
- grad_enc_up: float32 [768, 3072], P(('dp', 'fsdp'))
- grad_enc_down: float32 [3072, 768], P(('dp', 'fsdp'))
- grad_embedding: float32 [768, 512], P(('dp', 'fsdp'))
- grad_mask_token: float32 [512], P(('dp', 'fsdp'))
- grad_dec_gain1: float32 [512], P(('dp', 'fsdp'))
- grad_dec_shift1: float32 [512], P(('dp', 'fsdp'))
- grad_dec_qkv: float32 [512, 1536], P(('dp', 'fsdp'))
- grad_dec_proj: float32 [512, 512], P(('dp', 'fsdp'))
- grad_dec_gain2: float32 [512], P(('dp', 'fsdp'))
- grad_dec_shift2: float32 [512], P(('dp', 'fsdp'))
- grad_dec_up: float32 [512, 2048], P(('dp', 'fsdp'))
- grad_dec_down: float32 [2048, 512], P(('dp', 'fsdp'))
The draws below stay inside these ranges and needn't reach their ends.
Inputs may be any that keep to these rules, and one draw needn't show every extreme that they name: `bucket`: entry 0: the group holds five images of 196 patches with 49 kept each; entry 1: one image of 784 patches with 196 kept, then one small image; images lie end to end from row 0 as in the layout step. Both values occur in every draw. `keep_pos`: each encoder row of an image names a distinct decoder row of that same image; empty encoder rows hold 1024.
All inputs are finite; a program needn't handle non-finite values.
Results may differ from the reference program's by a relative error of at most 0.033.
Values may be sent and summed in bfloat16 or wider, within the bound.
No kernel may reach another device: no remote copies, remote signals or barrier semaphores. Data moves between devices by JAX's collectives and lax.ppermute only.
A program may use at most 320 MiB of HBM per device.

```python
import math
import jax
import jax.numpy as jnp
from jax import lax

WIDTH = 768
HIDDEN_SIZE = 3072
HEADS = 12
DEC_WIDTH = 512
DEC_HIDDEN = 2048
DEC_HEADS = 16
KEPT_SMALL = 49
ENC_ROWS = 256
DEC_ROWS = 1024
GROUPS_ALL = 32
ENC_TOKENS = 8192
DEC_TOKENS = 32768


def make_layout(key):
    bucket_key, small_key, large_key = jax.random.split(key, 3)
    draws = jax.random.randint(bucket_key, (GROUPS_ALL,), 0, 4)
    bucket_all = (draws == 0).astype(jnp.int32)
    bucket_all = bucket_all.at[0].set(1).at[1].set(0)
    patches = 4 * KEPT_SMALL
    small_perm = jax.vmap(lambda one_key: jax.random.permutation(one_key, patches))(jax.random.split(small_key, GROUPS_ALL * 5))
    small_perm = small_perm.reshape(GROUPS_ALL, 5, patches).astype(jnp.int32)
    large_perm = jax.vmap(lambda one_key: jax.random.permutation(one_key, 4 * patches))(jax.random.split(large_key, GROUPS_ALL))
    large_perm = large_perm.astype(jnp.int32)
    row_ids = jnp.arange(ENC_ROWS, dtype=jnp.int32)
    image = jnp.minimum(row_ids // KEPT_SMALL, 4)
    rank = row_ids % KEPT_SMALL
    small_pos = small_perm[:, image, rank] + image[None, :] * patches
    big_rank = jnp.minimum(row_ids, 4 * KEPT_SMALL - 1)
    tail_rank = jnp.clip(row_ids - 4 * KEPT_SMALL, 0, KEPT_SMALL - 1)
    big_pos = jnp.where(row_ids[None, :] < 4 * KEPT_SMALL, large_perm[:, big_rank], small_perm[:, 0, tail_rank] + 4 * patches)
    chosen = jnp.where(bucket_all[:, None] == 1, big_pos, small_pos)
    chosen = jnp.where(row_ids[None, :] < 5 * KEPT_SMALL, chosen, DEC_ROWS)
    return (bucket_all, chosen.astype(jnp.int32))


def draw_bucket(key, part):
    return make_layout(key)[0]


def draw_keep_pos(key, part):
    return make_layout(key)[1]


def shard_levels(own_key, dims, cuts, least, largest):
    loudness = 1.0
    for dim, shards_of in cuts:
        steps = jax.random.uniform(jax.random.fold_in(jax.random.fold_in(own_key, 6), dim), (shards_of,), jnp.float32, least / len(cuts), largest / len(cuts))
        loudness = loudness * jnp.repeat(jnp.exp(steps), dims[dim] // shards_of).reshape((-1,) + (1,) * (len(dims) - 1 - dim))
    return loudness


def noise(rng, extent, scale, limit, shards=(), kind=jnp.bfloat16):
    values = jax.random.normal(rng, extent, jnp.float32) * scale
    if len(shards) > 0:
        values = shard_levels(rng, extent, shards, -0.22, 0.18) * values
    return jnp.clip(values, min=-limit, max=limit).astype(kind)


def setup_inputs(seed: int = 0) -> dict:
    streams_of = jax.random.split(jax.random.key(seed), 23)
    tokens = noise(streams_of[0], (ENC_TOKENS, WIDTH), 1.0, 6.0, ((0, 32),))
    keep_pos = draw_keep_pos(jax.random.fold_in(streams_of[22], 71), 0)
    bucket = draw_bucket(jax.random.fold_in(streams_of[22], 71), 0)
    cotangent = noise(streams_of[3], (DEC_TOKENS, DEC_WIDTH), 1.0, 6.0, ((0, 32),))
    enc_gain1 = jnp.clip(1.0 + 0.1 * jax.random.normal(streams_of[4], (WIDTH,), jnp.float32), 0.5, 1.5).astype(jnp.bfloat16)
    enc_shift1 = noise(streams_of[5], (WIDTH,), 0.3, 2.0, ((0, 32),))
    enc_qkv = noise(streams_of[6], (WIDTH, 3 * WIDTH), (WIDTH // 2) ** -0.5, 0.3125, ((0, 32),))
    enc_proj = noise(streams_of[7], (WIDTH, WIDTH), (WIDTH // 8) ** -0.5, 0.625, ((0, 32),))
    enc_gain2 = jnp.clip(1.0 + 0.1 * jax.random.normal(streams_of[8], (WIDTH,), jnp.float32), 0.5, 1.5).astype(jnp.bfloat16)
    enc_shift2 = noise(streams_of[9], (WIDTH,), 0.3, 2.0, ((0, 32),))
    enc_up = noise(streams_of[10], (WIDTH, HIDDEN_SIZE), WIDTH ** -0.5, 0.21875, ((0, 32),))
    enc_down = noise(streams_of[11], (HIDDEN_SIZE, WIDTH), (HIDDEN_SIZE // 2) ** -0.5, 0.15625, ((0, 32),))
    embedding = noise(streams_of[12], (WIDTH, DEC_WIDTH), WIDTH ** -0.5, 0.21875, ((0, 32),))
    mask_token = noise(streams_of[13], (DEC_WIDTH,), 1.0, 4.0, ((0, 32),))
    dec_gain1 = jnp.clip(1.0 + 0.1 * jax.random.normal(streams_of[14], (DEC_WIDTH,), jnp.float32), 0.5, 1.5).astype(jnp.bfloat16)
    dec_shift1 = noise(streams_of[15], (DEC_WIDTH,), 0.3, 2.0, ((0, 32),))
    dec_qkv = noise(streams_of[16], (DEC_WIDTH, 3 * DEC_WIDTH), (DEC_WIDTH // 2) ** -0.5, 0.375, ((0, 32),))
    dec_proj = noise(streams_of[17], (DEC_WIDTH, DEC_WIDTH), (DEC_WIDTH // 8) ** -0.5, 0.75, ((0, 32),))
    dec_gain2 = jnp.clip(1.0 + 0.1 * jax.random.normal(streams_of[18], (DEC_WIDTH,), jnp.float32), 0.5, 1.5).astype(jnp.bfloat16)
    dec_shift2 = noise(streams_of[19], (DEC_WIDTH,), 0.3, 2.0, ((0, 32),))
    dec_up = noise(streams_of[20], (DEC_WIDTH, DEC_HIDDEN), DEC_WIDTH ** -0.5, 0.25, ((0, 32),))
    dec_down = noise(streams_of[21], (DEC_HIDDEN, DEC_WIDTH), (DEC_HIDDEN // 2) ** -0.5, 0.1875, ((0, 32),))
    return dict(tokens=tokens, keep_pos=keep_pos, bucket=bucket, cotangent=cotangent, enc_gain1=enc_gain1, enc_shift1=enc_shift1, enc_qkv=enc_qkv, enc_proj=enc_proj, enc_gain2=enc_gain2, enc_shift2=enc_shift2, enc_up=enc_up, enc_down=enc_down, embedding=embedding, mask_token=mask_token, dec_gain1=dec_gain1, dec_shift1=dec_shift1, dec_qkv=dec_qkv, dec_proj=dec_proj, dec_gain2=dec_gain2, dec_shift2=dec_shift2, dec_up=dec_up, dec_down=dec_down)


epsilon = 1e-06
highest = lax.Precision.HIGHEST

@jax.custom_vjp
def low(v):
    return lax.optimization_barrier(v.astype(jnp.bfloat16)).astype(jnp.float32)

@jax.custom_vjp
def low_back(v):
    return v

def low_keep(v):
    return (low(v), None)

def low_pass(kept, grad):
    return (grad,)

def back_keep(v):
    return (v, None)

def back_low(kept, grad):
    return (low(grad),)
low.defvjp(low_keep, low_pass)
low_back.defvjp(back_keep, back_low)

def enc_layout(bucket_row):
    row_ids = jnp.arange(ENC_ROWS, dtype=jnp.int32)[None, :]
    larger = bucket_row[:, None] == 1
    segment = jnp.where(larger, jnp.where(row_ids < 4 * KEPT_SMALL, 0, 1), row_ids // KEPT_SMALL)
    return jnp.where(row_ids < 5 * KEPT_SMALL, segment, 7)

def dec_layout(bucket_row):
    row_ids = jnp.arange(DEC_ROWS, dtype=jnp.int32)[None, :]
    patches = 4 * KEPT_SMALL
    larger = bucket_row[:, None] == 1
    first = row_ids < 4 * patches
    segment = jnp.where(larger, jnp.where(first, 0, 1), row_ids // patches)
    position = jnp.where(larger, jnp.where(first, row_ids, row_ids - 4 * patches), row_ids % patches)
    live_rows = row_ids < 5 * patches
    return (jnp.where(live_rows, segment, 7), position, live_rows)

def position_table(position, feature_count):
    column = jnp.arange(feature_count, dtype=jnp.int32)
    freq = jnp.exp((column // 2 * 2).astype(jnp.float32) * (-math.log(10000.0) / feature_count))
    angle = position[..., None].astype(jnp.float32) * freq
    return jnp.where(column % 2 == 0, jnp.sin(angle), jnp.cos(angle))

def layer_norm(hidden_in, gain, shift):
    centred = hidden_in - lax.optimization_barrier(jnp.mean(hidden_in, -1, keepdims=True))
    variance = lax.optimization_barrier(jnp.mean(centred * centred, -1, keepdims=True))
    return centred * lax.rsqrt(variance + epsilon) * gain + shift

def attend(act, w_qkv, w_proj, segment, heads):
    row_count, width = act.shape
    head_size = width // heads
    qkv = low(low_back(jnp.dot(low(act), w_qkv, precision=highest)))
    qkv = qkv.reshape(row_count, 3, heads, head_size)
    scores = jnp.einsum('qhd,khd->hqk', qkv[:, 0], qkv[:, 1], precision=highest) / math.sqrt(head_size)
    scores = low_back(scores)
    same = segment[:, None] == segment[None, :]
    scores = jnp.where(same[None], scores, -1e+30)
    row_max = lax.optimization_barrier(jnp.max(scores, -1, keepdims=True))
    weights = jnp.exp(scores - row_max)
    attn_prob = weights / lax.optimization_barrier(jnp.sum(weights, -1, keepdims=True))
    mixed_out = jnp.einsum('hqk,khd->qhd', low(attn_prob), qkv[:, 2], precision=highest)
    mixed_out = low(low_back(mixed_out.reshape(row_count, width)))
    return low_back(jnp.dot(mixed_out, w_proj, precision=highest))

def feed_forward(act, w_up, w_down):
    upward = low_back(jnp.dot(low(act), w_up, precision=highest))
    hidden_act = jax.nn.gelu(upward, approximate=False)
    return low_back(jnp.dot(low(hidden_act), w_down, precision=highest))

def residual_block(hidden_in, params, segment, heads):
    gain1, shift1, w_qkv, w_proj, gain2, shift2, w_up, w_down = params
    hidden_two = hidden_in + attend(layer_norm(hidden_in, gain1, shift1), w_qkv, w_proj, segment, heads)
    return hidden_two + feed_forward(layer_norm(hidden_two, gain2, shift2), w_up, w_down)

def group_forward(hidden_in, keep_row, bucket_one, params):
    enc_params = params[:8]
    embedding = params[8]
    mask_token = params[9]
    dec_params = params[10:]
    enc_seg = enc_layout(bucket_one[None])[0]
    dec_seg, position, live_rows = dec_layout(bucket_one[None])
    encoded = residual_block(hidden_in, enc_params, enc_seg, HEADS)
    small = low(low_back(jnp.dot(low(encoded), embedding, precision=highest)))
    onehot = (jnp.arange(DEC_ROWS, dtype=jnp.int32)[:, None] == keep_row[None, :]).astype(jnp.float32)
    kept_rows = lax.optimization_barrier(jnp.sum(onehot, 1, keepdims=True))
    dec_in = jnp.dot(onehot, small, precision=highest) + (1.0 - kept_rows) * mask_token + position_table(position[0], DEC_WIDTH)
    decoded = residual_block(dec_in, dec_params, dec_seg[0], DEC_HEADS)
    return decoded * live_rows[0][:, None].astype(jnp.float32)

def reference(tokens, keep_pos, bucket, cotangent, enc_gain1, enc_shift1, enc_qkv, enc_proj, enc_gain2, enc_shift2, enc_up, enc_down, embedding, mask_token, dec_gain1, dec_shift1, dec_qkv, dec_proj, dec_gain2, dec_shift2, dec_up, dec_down):
    weight_list = [enc_gain1, enc_shift1, enc_qkv, enc_proj, enc_gain2, enc_shift2, enc_up, enc_down, embedding, mask_token, dec_gain1, dec_shift1, dec_qkv, dec_proj, dec_gain2, dec_shift2, dec_up, dec_down]
    params = [weight.astype(jnp.float32) for weight in weight_list]
    hidden_all = tokens.astype(jnp.float32).reshape(GROUPS_ALL, ENC_ROWS, WIDTH)

    def forward(hidden_all, params):

        def per_group(items):
            return group_forward(items[0], items[1], items[2], params)
        return lax.map(jax.checkpoint(per_group), (hidden_all, keep_pos, bucket))
    result, pullback = jax.vjp(forward, hidden_all, params)
    grad_in, grads = pullback(cotangent.astype(jnp.float32).reshape(GROUPS_ALL, DEC_ROWS, DEC_WIDTH))
    return (result.reshape(DEC_TOKENS, DEC_WIDTH).astype(jnp.bfloat16), grad_in.reshape(ENC_TOKENS, WIDTH), grads[0], grads[1], grads[2], grads[3], grads[4], grads[5], grads[6], grads[7], grads[8], grads[9], grads[10], grads[11], grads[12], grads[13], grads[14], grads[15], grads[16], grads[17])
```

```python
import functools
import math

import jax
import jax.numpy as jnp
from jax import lax
from jax.experimental import pallas as pl
from jax.experimental.pallas import tpu as pltpu
from jax.sharding import PartitionSpec as P

HEADS = 12
DEC_WIDTH = 512
DEC_HEADS = 16
KEPT_SMALL = 49
ENC_ROWS = 256
DEC_ROWS = 1024


epsilon = 1e-06


NEG = -1e30
LANES = 128
LOG2E = 1.4426950408889634
VMEM_LIMIT = 56 * 1024 * 1024

def nt(a, b):
    return lax.dot_general(a, b, (((1,), (1,)), ((), ())), preferred_element_type=jnp.float32)

def nn(a, b):
    return lax.dot_general(a, b, (((1,), (0,)), ((), ())), preferred_element_type=jnp.float32)

def iota(shape, dim):
    return lax.broadcasted_iota(jnp.int32, shape, dim)

def dec_fwd_kernel(bucket_ref, qkv_ref, o_ref, lse_ref, stat, *, heads, size, small):
    width = heads * size
    per = LANES // size
    c = LOG2E / math.sqrt(size)
    lane = iota((1, LANES), 1)
    big = 4 * small
    live = 5 * small

    def tile(g, q0, nq, k0, nk, mask):
        q = qkv_ref[pl.ds(q0, nq), pl.ds(g * LANES, LANES)]
        k = qkv_ref[pl.ds(k0, nk), pl.ds(width + g * LANES, LANES)]
        v = qkv_ref[pl.ds(k0, nk), pl.ds(2 * width + g * LANES, LANES)]
        acc = jnp.zeros((nq, LANES), jnp.float32)
        st = stat[pl.ds(q0, nq), :]
        for h in range(per):
            mine = (lane // size) == h
            s = mask(nt(jnp.where(mine, q, jnp.zeros_like(q)), k))
            top = jnp.max(s, -1, keepdims=True)
            p = jnp.exp2((s - top) * c)
            total = jnp.sum(p, -1, keepdims=True)
            acc = acc + nn(p.astype(jnp.bfloat16), jnp.where(mine, v, jnp.zeros_like(v))) * (1.0 / total)
            st = jnp.where(lane == g * 8 + h, top * c + jnp.log2(total), st)
        o_ref[pl.ds(q0, nq), pl.ds(g * LANES, LANES)] = acc.astype(jnp.bfloat16)
        stat[pl.ds(q0, nq), :] = st

    def seg_mask(q0, k0, seg):
        def f(s):
            rows = iota((s.shape[0], 1), 0) + q0
            cols = iota((1, s.shape[1]), 1) + k0
            return jnp.where(seg(rows) == seg(cols), s, NEG)
        return f

    @pl.when(bucket_ref[0] == 1)
    def _():
        def tail_mask(s):
            tail = jnp.where(iota((1, LANES), 1) < 16, s[:, 768:], NEG)
            return jnp.concatenate([s[:, :768], tail], 1)

        def one(g, _):
            tile(g, 0, 784, 0, 896, tail_mask)
            tile(g, 784, 240, 768, 256, seg_mask(784, 768, lambda r: jnp.where(r < big, 0, jnp.where(r < live, 1, 7))))
            return 0
        lax.fori_loop(0, width // LANES, one, 0)

    @pl.when(bucket_ref[0] != 1)
    def _():
        def one(i, _):
            g = i // 4
            t = i % 4
            q0 = pl.multiple_of(t * 256, 256)
            k0 = pl.multiple_of(jnp.where(t == 0, 0, jnp.where(t == 1, 128, jnp.where(t == 2, 384, 512))), 128)
            tile(g, q0, 256, k0, 512, seg_mask(q0, k0, lambda r: jnp.where(r < live, r // small, 7)))
            return 0
        lax.fori_loop(0, 4 * (width // LANES), one, 0)

    lse_ref[...] = stat[...].T[:8 * (width // LANES), :]

def dec_fwd(qkv, bucket, heads, size, small):
    rows = qkv.shape[0]
    width = heads * size
    return pl.pallas_call(
        functools.partial(dec_fwd_kernel, heads=heads, size=size, small=small),
        out_shape=(jax.ShapeDtypeStruct((rows, width), jnp.bfloat16), jax.ShapeDtypeStruct((8 * (width // LANES), rows), jnp.float32)),
        in_specs=[pl.BlockSpec(memory_space=pltpu.SMEM), pl.BlockSpec(memory_space=pltpu.VMEM)],
        out_specs=(pl.BlockSpec(memory_space=pltpu.VMEM), pl.BlockSpec(memory_space=pltpu.VMEM)),
        scratch_shapes=[pltpu.VMEM((rows, LANES), jnp.float32)],
        compiler_params=pltpu.CompilerParams(vmem_limit_bytes=VMEM_LIMIT),
    )(bucket, qkv)

def dec_bwd_kernel(bucket_ref, qkv_ref, go_ref, o_ref, lse_ref, g_ref, gq_ref, gk_ref, gv_ref, dl_ref, *, heads, size, small):
    width = heads * size
    per = LANES // size
    rows = qkv_ref.shape[0]
    scale = 1.0 / math.sqrt(size)
    c = LOG2E * scale
    lane = iota((1, LANES), 1)
    big = 4 * small
    live = 5 * small

    slots = 8 * (width // LANES)
    feat = iota((slots, width), 1)
    slot = iota((slots, width), 0)
    ind = (feat // LANES * 8 + feat % LANES // size == slot).astype(jnp.float32)
    prod = go_ref[...].astype(jnp.float32) * o_ref[...].astype(jnp.float32)
    dl_ref[...] = lax.dot_general(ind, prod, (((1,), (1,)), ((), ())), preferred_element_type=jnp.float32, precision=lax.Precision.HIGHEST)

    gk_ref[...] = jnp.zeros_like(gk_ref)
    gv_ref[...] = jnp.zeros_like(gv_ref)
    gq_ref[...] = jnp.zeros_like(gq_ref)

    def tile(g, q0, nq, k0, nk, lanes_ok, mask):
        q = qkv_ref[pl.ds(q0, nq), pl.ds(g * LANES, LANES)]
        k = qkv_ref[pl.ds(k0, nk), pl.ds(width + g * LANES, LANES)]
        v = qkv_ref[pl.ds(k0, nk), pl.ds(2 * width + g * LANES, LANES)]
        go = go_ref[pl.ds(q0, nq), pl.ds(g * LANES, LANES)]
        kt = k.T
        gk = jnp.zeros((nk, LANES), jnp.float32)
        gv = jnp.zeros((nk, LANES), jnp.float32)
        gqs = []
        lse4 = lse_ref[pl.ds(pl.multiple_of(g * 8, 8), 8), pl.ds(q0, nq)]
        dl4 = dl_ref[pl.ds(pl.multiple_of(g * 8, 8), 8), pl.ds(q0, nq)]
        for h in range(per):
            mine = (lane // size) == h
            qm = jnp.where(mine, q, jnp.zeros_like(q))
            gom = jnp.where(mine, go, jnp.zeros_like(go))
            lse = lse4[h:h + 1]
            if lanes_ok is not None:
                lse = jnp.where(lanes_ok(iota((1, nq), 1) + q0), lse, -NEG)
            s = nt(k, qm)
            p = jnp.exp2(s * c - lse)
            if mask is not None:
                p = mask(p)
            dp = nt(v, gom)
            ds = (p * (dp - dl4[h:h + 1])).astype(jnp.bfloat16)
            gv = gv + nn(p.astype(jnp.bfloat16), gom)
            gk = gk + nn(ds, qm)
            gqs.append(nn(kt[h * size:(h + 1) * size], ds))
        gk_ref[pl.ds(k0, nk), pl.ds(g * LANES, LANES)] += gk
        gv_ref[pl.ds(k0, nk), pl.ds(g * LANES, LANES)] += gv
        gq_ref[pl.ds(g * LANES, LANES), pl.ds(q0, nq)] += jnp.concatenate(gqs, 0)

    def seg_mask(q0, k0, seg):
        def f(p):
            rows_ = iota((p.shape[0], 1), 0) + k0
            cols = iota((1, p.shape[1]), 1) + q0
            return jnp.where(seg(rows_) == seg(cols), p, 0.0)
        return f

    @pl.when(bucket_ref[0] == 1)
    def _():
        def one(i, _):
            g = i // 3
            tile(g, pl.multiple_of((i % 3) * 256, 256), 256, 0, 784, None, None)
            return 0
        lax.fori_loop(0, 3 * (width // LANES), one, 0)
        def two(g, _):
            tile(g, 768, 128, 0, 784, lambda r: r < big, None)
            tile(g, 768, 256, 784, 240, None, seg_mask(768, 784, lambda r: jnp.where(r < big, 0, jnp.where(r < live, 1, 7))))
            return 0
        lax.fori_loop(0, width // LANES, two, 0)

    @pl.when(bucket_ref[0] != 1)
    def _():
        def one(i, _):
            g = i // 4
            t = i % 4
            q0 = pl.multiple_of(t * 256, 256)
            k0 = pl.multiple_of(jnp.where(t == 0, 0, jnp.where(t == 1, 128, jnp.where(t == 2, 384, 512))), 128)
            tile(g, q0, 256, k0, 512, None, seg_mask(q0, k0, lambda r: jnp.where(r < live, r // small, 7)))
            return 0
        lax.fori_loop(0, 4 * (width // LANES), one, 0)

    g_ref[:, 0:width] = (gq_ref[...].T * scale).astype(jnp.bfloat16)
    g_ref[:, width:2 * width] = (gk_ref[...] * scale).astype(jnp.bfloat16)
    g_ref[:, 2 * width:] = gv_ref[...].astype(jnp.bfloat16)

def dec_bwd(qkv, go, o, lse, bucket, heads, size, small):
    rows = qkv.shape[0]
    width = heads * size
    V = pl.BlockSpec(memory_space=pltpu.VMEM)
    return pl.pallas_call(
        functools.partial(dec_bwd_kernel, heads=heads, size=size, small=small),
        out_shape=jax.ShapeDtypeStruct((rows, 3 * width), jnp.bfloat16),
        in_specs=[pl.BlockSpec(memory_space=pltpu.SMEM), V, V, V, V],
        out_specs=V,
        scratch_shapes=[pltpu.VMEM((width, rows), jnp.float32), pltpu.VMEM((rows, width), jnp.float32), pltpu.VMEM((rows, width), jnp.float32), pltpu.VMEM((8 * (width // LANES), rows), jnp.float32)],
        compiler_params=pltpu.CompilerParams(vmem_limit_bytes=VMEM_LIMIT),
    )(bucket, qkv, go, o, lse)

def group_map(one, bucket, *arrays):
    groups = bucket.shape[0]
    outs = []
    for g in range(groups):
        cut = [a[g * (a.shape[0] // groups) : (g + 1) * (a.shape[0] // groups)] for a in arrays]
        outs.append(one(*cut, bucket[g : g + 1]))
    if groups == 1:
        return outs[0]
    return tuple(jnp.concatenate(parts, 0) for parts in zip(*outs))


def enc_layout(bucket_row):
    row_ids = jnp.arange(ENC_ROWS, dtype=jnp.int32)[None, :]
    larger = bucket_row[:, None] == 1
    segment = jnp.where(larger, jnp.where(row_ids < 4 * KEPT_SMALL, 0, 1), row_ids // KEPT_SMALL)
    return jnp.where(row_ids < 5 * KEPT_SMALL, segment, 7)


def dec_layout(bucket_row):
    row_ids = jnp.arange(DEC_ROWS, dtype=jnp.int32)[None, :]
    patches = 4 * KEPT_SMALL
    larger = bucket_row[:, None] == 1
    first = row_ids < 4 * patches
    segment = jnp.where(larger, jnp.where(first, 0, 1), row_ids // patches)
    position = jnp.where(
        larger, jnp.where(first, row_ids, row_ids - 4 * patches), row_ids % patches
    )
    live_rows = row_ids < 5 * patches
    return (jnp.where(live_rows, segment, 7), position, live_rows)


def position_table(position, feature_count):
    column = jnp.arange(feature_count, dtype=jnp.int32)
    freq = jnp.exp((column // 2 * 2).astype(jnp.float32) * (-math.log(10000.0) / feature_count))
    angle = position[..., None].astype(jnp.float32) * freq
    return jnp.where(column % 2 == 0, jnp.sin(angle), jnp.cos(angle))


def contract_rows(left, right):
    return lax.dot_general(
        left, right, (((0,), (0,)), ((), ())), preferred_element_type=jnp.float32
    )


def times_transposed(left, weight):
    return lax.dot_general(
        left, weight, (((1,), (1,)), ((), ())), preferred_element_type=jnp.float32
    )


def norm_forward(hidden_in, gain, shift):
    centred = hidden_in - jnp.mean(hidden_in, -1, keepdims=True)
    inv_std = lax.rsqrt(jnp.mean(centred * centred, -1, keepdims=True) + epsilon)
    normed = centred * inv_std
    return (normed * gain + shift, normed, inv_std)


def norm_backward(grad, normed, inv_std, gain):
    grad_gain = jnp.sum(grad * normed, 0)
    grad_shift = jnp.sum(grad, 0)
    grad_norm = grad * gain
    grad_in = inv_std * (
        grad_norm
        - jnp.mean(grad_norm, -1, keepdims=True)
        - normed * jnp.mean(grad_norm * normed, -1, keepdims=True)
    )
    return (grad_in, grad_gain, grad_shift)


def block_shape(segment):
    row_count = segment.shape[1]
    span = row_count if row_count % 512 else 512
    return (segment.shape[0], row_count, span, row_count // span)


def masked_scores(queries, key_rows, segment, group_at, offset, span, scale):
    seg_all = lax.dynamic_index_in_dim(segment, group_at, 0, keepdims=False)
    seg_query = lax.dynamic_slice_in_dim(seg_all, offset, span, 0)
    scores = (
        jnp.einsum("qhd,khd->hqk", queries, key_rows, preferred_element_type=jnp.float32) * scale
    )
    return jnp.where((seg_query[:, None] == seg_all[None, :])[None], scores, -1e30)


def attend_forward(qkv_r, segment, heads):
    width = qkv_r.shape[1] // 3
    head_size = width // heads
    groups, row_count, span, part_count = block_shape(segment)
    qkv_grid = qkv_r.reshape(groups, row_count, 3, heads, head_size)
    scale = 1.0 / math.sqrt(head_size)

    def forward_block(which):
        group_at = which // part_count
        offset = which % part_count * span
        local_qkv = lax.dynamic_index_in_dim(qkv_grid, group_at, 0, keepdims=False)
        queries = lax.dynamic_slice_in_dim(local_qkv[:, 0], offset, span, 0)
        scores = masked_scores(queries, local_qkv[:, 1], segment, group_at, offset, span, scale)
        row_max = jnp.max(scores, -1, keepdims=True)
        weights = jnp.exp(scores - row_max)
        denom_sum = jnp.sum(weights, -1, keepdims=True)
        attn_prob = (weights / denom_sum).astype(jnp.bfloat16)
        mixed_out = jnp.einsum(
            "hqk,khd->qhd", attn_prob, local_qkv[:, 2], preferred_element_type=jnp.float32
        )
        return (mixed_out.reshape(span, width), (row_max + jnp.log(denom_sum))[:, :, 0])

    mixed_out, log_total = lax.map(forward_block, jnp.arange(groups * part_count))
    return (mixed_out.reshape(groups * row_count, width), log_total)


def attend_backward(qkv_r, segment, log_total, grad_mixed, heads):
    width = qkv_r.shape[1] // 3
    head_size = width // heads
    groups, row_count, span, part_count = block_shape(segment)
    qkv_grid = qkv_r.reshape(groups, row_count, 3, heads, head_size)
    grad_grid = grad_mixed.reshape(groups, row_count, heads, head_size)
    scale = 1.0 / math.sqrt(head_size)

    def backward_block(which):
        group_at = which // part_count
        offset = which % part_count * span
        local_qkv = lax.dynamic_index_in_dim(qkv_grid, group_at, 0, keepdims=False)
        queries = lax.dynamic_slice_in_dim(local_qkv[:, 0], offset, span, 0)
        grad_rows = lax.dynamic_slice_in_dim(
            lax.dynamic_index_in_dim(grad_grid, group_at, 0, keepdims=False), offset, span, 0
        )
        scores = masked_scores(queries, local_qkv[:, 1], segment, group_at, offset, span, scale)
        attn_prob = jnp.exp(scores - log_total[which][:, :, None])
        grad_prob = jnp.einsum(
            "qhd,khd->hqk", grad_rows, local_qkv[:, 2], preferred_element_type=jnp.float32
        )
        grad_score = (
            attn_prob * (grad_prob - jnp.sum(grad_prob * attn_prob, -1, keepdims=True))
        ).astype(jnp.bfloat16)
        grad_query = (
            jnp.einsum(
                "hqk,khd->qhd", grad_score, local_qkv[:, 1], preferred_element_type=jnp.float32
            )
            * scale
        )
        grad_key = (
            jnp.einsum("hqk,qhd->khd", grad_score, queries, preferred_element_type=jnp.float32)
            * scale
        )
        grad_value = jnp.einsum(
            "hqk,qhd->khd",
            attn_prob.astype(jnp.bfloat16),
            grad_rows,
            preferred_element_type=jnp.float32,
        )
        return (grad_query, grad_key, grad_value)

    grad_query, grad_key, grad_value = lax.map(backward_block, jnp.arange(groups * part_count))
    grad_query = grad_query.reshape(groups, row_count, heads, head_size)
    grad_key = jnp.sum(grad_key.reshape(groups, part_count, row_count, heads, head_size), 1)
    grad_value = jnp.sum(grad_value.reshape(groups, part_count, row_count, heads, head_size), 1)
    stacked = jnp.stack([grad_query, grad_key, grad_value], 2)
    return stacked.reshape(groups * row_count, 3 * width).astype(jnp.bfloat16)


def block_forward(hidden_in, weights, segment, heads):
    gain1, shift1, w_qkv, w_proj, gain2, shift2, w_up, w_down = weights
    act_one, normed_one, inv_one = norm_forward(
        hidden_in, gain1.astype(jnp.float32), shift1.astype(jnp.float32)
    )
    act_one = act_one.astype(jnp.bfloat16)
    qkv_r = jnp.dot(act_one, w_qkv, preferred_element_type=jnp.float32).astype(jnp.bfloat16)
    if segment.ndim == 1:
        mixed_out, log_total = group_map(
            lambda rows, which: dec_fwd(rows, which, heads, qkv_r.shape[1] // 3 // heads, 4 * KEPT_SMALL),
            segment,
            qkv_r,
        )
    else:
        mixed_out, log_total = attend_forward(qkv_r, segment, heads)
        mixed_out = mixed_out.astype(jnp.bfloat16)
    hidden_two = hidden_in + jnp.dot(mixed_out, w_proj, preferred_element_type=jnp.float32)
    act_two, normed_two, inv_two = norm_forward(
        hidden_two, gain2.astype(jnp.float32), shift2.astype(jnp.float32)
    )
    act_two = act_two.astype(jnp.bfloat16)
    upward = jnp.dot(act_two, w_up, preferred_element_type=jnp.float32)
    hidden_act = jax.nn.gelu(upward, approximate=False).astype(jnp.bfloat16)
    result = hidden_two + jnp.dot(hidden_act, w_down, preferred_element_type=jnp.float32)
    saved = (
        normed_one,
        inv_one,
        act_one,
        qkv_r,
        log_total,
        mixed_out,
        normed_two,
        inv_two,
        act_two,
        upward,
        hidden_act,
    )
    return (result, saved)


def block_backward(grad, weights, saved, segment, heads):
    gain1, shift1, w_qkv, w_proj, gain2, shift2, w_up, w_down = weights
    (
        normed_one,
        inv_one,
        act_one,
        qkv_r,
        log_total,
        mixed_out,
        normed_two,
        inv_two,
        act_two,
        upward,
        hidden_act,
    ) = saved
    grad_r = grad.astype(jnp.bfloat16)
    grad_down = contract_rows(hidden_act, grad_r)
    grad_hidden = times_transposed(grad_r, w_down)
    unused, gelu_pull = jax.vjp(lambda values: jax.nn.gelu(values, approximate=False), upward)
    grad_upward = gelu_pull(grad_hidden)[0].astype(jnp.bfloat16)
    grad_up = contract_rows(act_two, grad_upward)
    grad_act_two = times_transposed(grad_upward, w_up)
    grad_two, grad_gain2, grad_shift2 = norm_backward(
        grad_act_two, normed_two, inv_two, gain2.astype(jnp.float32)
    )
    grad_two = grad_two + grad
    grad_two_r = grad_two.astype(jnp.bfloat16)
    grad_proj = contract_rows(mixed_out, grad_two_r)
    grad_mixed = times_transposed(grad_two_r, w_proj).astype(jnp.bfloat16)
    if segment.ndim == 1:
        (grad_qkv_r,) = group_map(
            lambda rows, back, mixed, total, which: (
                dec_bwd(rows, back, mixed, total, which, heads, qkv_r.shape[1] // 3 // heads, 4 * KEPT_SMALL),
            ),
            segment,
            qkv_r,
            grad_mixed,
            mixed_out,
            log_total,
        )
    else:
        grad_qkv_r = attend_backward(qkv_r, segment, log_total, grad_mixed, heads)
    grad_qkv = contract_rows(act_one, grad_qkv_r)
    grad_act_one = times_transposed(grad_qkv_r, w_qkv)
    grad_one, grad_gain1, grad_shift1 = norm_backward(
        grad_act_one, normed_one, inv_one, gain1.astype(jnp.float32)
    )
    return (
        grad_one + grad_two,
        (grad_gain1, grad_shift1, grad_qkv, grad_proj, grad_gain2, grad_shift2, grad_up, grad_down),
    )


def exchange(values, mask):
    outer = lax.axis_size("dp")
    inner = lax.axis_size("fsdp")
    return lax.ppermute(
        values, ("dp", "fsdp"), [(i, i ^ mask) for i in range(outer * inner)]
    )


def reduce_rows(values, order):
    inner = lax.axis_size("fsdp")
    me = lax.axis_index("dp") * inner + lax.axis_index("fsdp")
    left = sorted(order, reverse=True)
    cols = values.shape[1:]
    for mask in order:
        at = left.index(mask)
        before = 2**at
        rows = values.shape[0] // (2 * before)
        view = values.reshape((before, 2, rows) + cols)
        bit = (me // mask) % 2
        keep = lax.dynamic_index_in_dim(view, bit, 1, keepdims=False)
        send = lax.dynamic_index_in_dim(view, 1 - bit, 1, keepdims=False)
        arrived = exchange(send.reshape((before * rows,) + cols), mask)
        keep = keep.reshape((before * rows,) + cols)
        values = (keep.astype(jnp.float32) + arrived.astype(jnp.float32)).astype(jnp.bfloat16)
        left.remove(mask)
    return values


def bit_masks(low, high):
    masks = []
    while low < high:
        masks.append(low)
        low *= 2
    return masks


def gather(values):
    return lax.all_gather(values, ("dp", "fsdp"), axis=0, tiled=True)


def pad_lanes(vectors):
    stacked = jnp.stack(vectors, 1)
    return jnp.pad(stacked, ((0, 0), (0, 128 - stacked.shape[1])))


def wide(values, parts):
    rows = values.shape[0] // parts
    return jnp.concatenate([values[i * rows : (i + 1) * rows] for i in range(parts)], 1)


def tall(values, devices, parts):
    rows = values.shape[0] // devices
    cols = values.shape[1] // parts
    grid = values.reshape(devices, rows, parts, cols)
    return jnp.transpose(grid, (0, 2, 1, 3)).reshape(devices * parts * rows, cols)


def shards(
    tokens,
    keep_pos,
    bucket,
    cotangent,
    enc_gain1,
    enc_shift1,
    enc_qkv,
    enc_proj,
    enc_gain2,
    enc_shift2,
    enc_up,
    enc_down,
    embedding,
    mask_token,
    dec_gain1,
    dec_shift1,
    dec_qkv,
    dec_proj,
    dec_gain2,
    dec_shift2,
    dec_up,
    dec_down,
):
    devices = lax.axis_size("dp") * lax.axis_size("fsdp")
    inner = lax.axis_size("fsdp")
    enc_width = tokens.shape[1]
    enc_pack = jnp.concatenate(
        [
            enc_qkv,
            enc_proj,
            enc_up,
            wide(enc_down, 4),
            embedding,
            pad_lanes([enc_gain1, enc_shift1, enc_gain2, enc_shift2]),
        ],
        1,
    )
    dec_pack = jnp.concatenate(
        [
            dec_qkv,
            dec_proj,
            dec_up,
            wide(dec_down, 4),
            pad_lanes([dec_gain1, dec_shift1, dec_gain2, dec_shift2, mask_token]),
        ],
        1,
    )
    enc_all = gather(enc_pack)
    dec_all = gather(dec_pack)

    def unpack(values, width, hidden):
        at = 0
        parts = []
        for cols in (3 * width, width, hidden, hidden):
            parts.append(values[:, at : at + cols])
            at += cols
        parts[3] = tall(parts[3], devices, 4)
        return parts, values[:, at:]

    enc_parts, enc_rest = unpack(enc_all, enc_width, enc_up.shape[1])
    dec_parts, dec_rest = unpack(dec_all, DEC_WIDTH, dec_up.shape[1])
    embed = enc_rest[:, :DEC_WIDTH]
    enc_vec = enc_rest[:, DEC_WIDTH:]
    enc_full = (
        enc_vec[:, 0],
        enc_vec[:, 1],
        enc_parts[0],
        enc_parts[1],
        enc_vec[:, 2],
        enc_vec[:, 3],
        enc_parts[2],
        enc_parts[3],
    )
    dec_full = (
        dec_rest[:, 0],
        dec_rest[:, 1],
        dec_parts[0],
        dec_parts[1],
        dec_rest[:, 2],
        dec_rest[:, 3],
        dec_parts[2],
        dec_parts[3],
    )
    mask_full = dec_rest[:, 4]
    groups = bucket.shape[0]
    enc_seg = enc_layout(bucket)
    dec_seg, position, live_rows = dec_layout(bucket)
    encoded, enc_saved = block_forward(tokens.astype(jnp.float32), enc_full, enc_seg, HEADS)
    encoded_r = encoded.astype(jnp.bfloat16)
    small = jnp.dot(encoded_r, embed, preferred_element_type=jnp.float32).astype(jnp.bfloat16)
    onehot = (jnp.arange(DEC_ROWS, dtype=jnp.int32)[None, :, None] == keep_pos[:, None, :]).astype(
        jnp.bfloat16
    )
    kept_rows = jnp.sum(onehot.astype(jnp.float32), 2, keepdims=True)
    placed = jnp.einsum(
        "gde,gew->gdw",
        onehot,
        small.reshape(groups, ENC_ROWS, DEC_WIDTH),
        preferred_element_type=jnp.float32,
    )
    mask_row = mask_full.astype(jnp.float32)
    dec_in = placed + (1.0 - kept_rows) * mask_row + position_table(position, DEC_WIDTH)
    dec_in = dec_in.reshape(groups * DEC_ROWS, DEC_WIDTH)
    decoded, dec_saved = block_forward(dec_in, dec_full, bucket, DEC_HEADS)
    live_float = live_rows.reshape(groups * DEC_ROWS, 1).astype(jnp.float32)
    output = (decoded * live_float).astype(jnp.bfloat16)
    grad_dec, dec_grads = block_backward(
        cotangent.astype(jnp.float32) * live_float, dec_full, dec_saved, bucket, DEC_HEADS
    )
    grad_grid = grad_dec.reshape(groups, DEC_ROWS, DEC_WIDTH)
    grad_mask = jnp.sum(grad_grid * (1.0 - kept_rows), (0, 1))

    cols_low = bit_masks(inner, devices)
    lines = bit_masks(2, inner)
    first = [1] + cols_low + lines
    second = [1] + cols_low[::-1] + lines
    third = [1] + lines + cols_low

    def reduced(matrix, order):
        return reduce_rows(matrix.astype(jnp.bfloat16), order).astype(jnp.float32)

    gain1, shift1, g_qkv, g_proj, gain2, shift2, g_up, g_down = dec_grads
    dec_a = jnp.concatenate([g_up, g_proj, pad_lanes([gain1, shift1, gain2, shift2, grad_mask])], 1)
    dec_a = reduced(dec_a, first)
    g_dec_down = reduced(g_down, second)
    g_dec_qkv = reduced(g_qkv, third)
    hidden = g_up.shape[1]
    g_dec_up = dec_a[:, :hidden]
    g_dec_proj = dec_a[:, hidden : hidden + DEC_WIDTH]
    dec_vecs = [dec_a[:, hidden + DEC_WIDTH + i] for i in range(5)]

    safe_rows = jnp.minimum(keep_pos, DEC_ROWS - 1)
    picked = jnp.take_along_axis(grad_grid, safe_rows[:, :, None], 1)
    grad_small = (
        jnp.where((keep_pos < DEC_ROWS)[:, :, None], picked, 0.0)
        .astype(jnp.bfloat16)
        .reshape(groups * ENC_ROWS, DEC_WIDTH)
    )
    grad_embedding = contract_rows(encoded_r, grad_small)
    grad_encoded = times_transposed(grad_small, embed)
    grad_tokens, enc_grads = block_backward(grad_encoded, enc_full, enc_saved, enc_seg, HEADS)
    gain1, shift1, g_qkv, g_proj, gain2, shift2, g_up, g_down = enc_grads
    g_enc_down = reduced(g_down, first)
    enc_b = jnp.concatenate([g_up, grad_embedding], 1)
    enc_b = reduced(enc_b, second)
    enc_c = jnp.concatenate([g_qkv, g_proj, pad_lanes([gain1, shift1, gain2, shift2])], 1)
    enc_c = reduced(enc_c, third)
    hidden = g_up.shape[1]
    g_enc_up = enc_b[:, :hidden]
    g_embedding = enc_b[:, hidden:]
    g_enc_qkv = enc_c[:, : 3 * enc_width]
    g_enc_proj = enc_c[:, 3 * enc_width : 4 * enc_width]
    enc_vecs = [enc_c[:, 4 * enc_width + i] for i in range(4)]
    return (
        output,
        grad_tokens,
        enc_vecs[0],
        enc_vecs[1],
        g_enc_qkv,
        g_enc_proj,
        enc_vecs[2],
        enc_vecs[3],
        g_enc_up,
        g_enc_down,
        g_embedding,
        dec_vecs[4],
        dec_vecs[0],
        dec_vecs[1],
        g_dec_qkv,
        g_dec_proj,
        dec_vecs[2],
        dec_vecs[3],
        g_dec_up,
        g_dec_down,
    )


def solution(mesh):
    in_specs = (
        P(("dp", "fsdp"), None),
        P(("dp", "fsdp"), None),
        P(("dp", "fsdp")),
        P(("dp", "fsdp"), None),
        P(("dp", "fsdp")),
        P(("dp", "fsdp")),
        P(("dp", "fsdp"), None),
        P(("dp", "fsdp"), None),
        P(("dp", "fsdp")),
        P(("dp", "fsdp")),
        P(("dp", "fsdp"), None),
        P(("dp", "fsdp"), None),
        P(("dp", "fsdp"), None),
        P(("dp", "fsdp")),
        P(("dp", "fsdp")),
        P(("dp", "fsdp")),
        P(("dp", "fsdp"), None),
        P(("dp", "fsdp"), None),
        P(("dp", "fsdp")),
        P(("dp", "fsdp")),
        P(("dp", "fsdp"), None),
        P(("dp", "fsdp"), None),
    )
    out_specs = (
        P(("dp", "fsdp"), None),
        P(("dp", "fsdp"), None),
        P(("dp", "fsdp")),
        P(("dp", "fsdp")),
        P(("dp", "fsdp"), None),
        P(("dp", "fsdp"), None),
        P(("dp", "fsdp")),
        P(("dp", "fsdp")),
        P(("dp", "fsdp"), None),
        P(("dp", "fsdp"), None),
        P(("dp", "fsdp"), None),
        P(("dp", "fsdp")),
        P(("dp", "fsdp")),
        P(("dp", "fsdp")),
        P(("dp", "fsdp"), None),
        P(("dp", "fsdp"), None),
        P(("dp", "fsdp")),
        P(("dp", "fsdp")),
        P(("dp", "fsdp"), None),
        P(("dp", "fsdp"), None),
    )
    return jax.shard_map(shards, mesh=mesh, in_specs=in_specs, out_specs=out_specs, check_vma=False)
```
